32 devices in a mesh: src: 8 (over z, y), rcv: 4 (over x, core).
Axes of the slice: x: 2, y: 2, z: 4, core: 2. Of those that a mesh axis runs over, the one named last changes fastest.
Arguments:
- src_coords: float32 [3, 16], P(None, 'src'), may hold values from -1 to 1
- rcv_coords: float32 [3, 16, 2048], P(None, 'src', 'rcv'), may hold values from -1 to 1
- velocity: float32 [16, 2048], P('src', 'rcv'), may hold values from 0.5 to 2
- pair_mask: int32 [16, 2048], P('src', 'rcv'), may hold values from 0 to 1, as said below
- near_flag: int32 [16, 2048], P('src', 'rcv'), may hold values 0 or 1
- block_params: float32 [2048, 512], P(('src', 'rcv')), may hold values from -0.25 to 0.25
- edge_params: float32 [6144], P(('src', 'rcv'))
- block_moment: float32 [2048, 512], P(('src', 'rcv')), may hold values from -0.0007324219 to 0.0007324219
- edge_moment: float32 [6144], P(('src', 'rcv')), may hold values from -0.001953125 to 0.001953125
- block_second: float32 [2048, 512], P(('src', 'rcv')), may hold values from 2.3702973e-09 to 9.481189e-09
- edge_second: float32 [6144], P(('src', 'rcv')), may hold values from 2.1332676e-08 to 8.5330704e-08
Outputs:
- grad_norm: float32 [], replicated
- new_blocks: float32 [2048, 512], P(('src', 'rcv'))
- new_edges: float32 [6144], P(('src', 'rcv'))
- moment_blocks: float32 [2048, 512], P(('src', 'rcv'))
- moment_edges: float32 [6144], P(('src', 'rcv'))
- second_blocks: float32 [2048, 512], P(('src', 'rcv'))
- second_edges: float32 [6144], P(('src', 'rcv'))
- low_blocks: bfloat16 [2048, 512], P(('src', 'rcv'))
- low_edges: bfloat16 [6144], P(('src', 'rcv'))
The draws below stay inside these ranges and needn't reach their ends.
Inputs may be any that keep to these rules, and one draw needn't show every extreme that they name: `pair_mask`: 1 marks a pair that enters the loss.
All inputs are finite; a program needn't handle non-finite values. No bound on the sum of `near_flag` on one device may be relied on, other than what follows from the above.
Results may differ from the reference program's by a relative error of at most 0.001.
Values sent between devices are 32-bit elements; how exact they have to be, the bound alone decides.
No kernel may reach another device: no remote copies, remote signals or barrier semaphores. Data moves between devices by JAX's collectives and lax.ppermute only.
A program may use at most 320 MiB of HBM per device.

```python
import math
import jax
import jax.numpy as jnp
from jax import lax

D = 512
ADAM_STEP = 5
NSRC = 16
NRCV = 2048


def draw_pair_mask(key, part):
    key = jax.random.fold_in(key, 1)
    scores = jax.random.randint(key, (NSRC, NRCV), 0, 3 * NSRC * NRCV)
    src_pos = jnp.arange(NSRC, dtype=jnp.int32)[:, None]
    rcv_pos = jnp.arange(NRCV, dtype=jnp.int32)[None, :]
    limit = NSRC * NRCV + src_pos * NRCV + rcv_pos * NSRC
    return (scores < limit).astype(jnp.int32)


def draw_edge_params(key, part):
    key = jax.random.fold_in(key, 2)
    values = jax.random.normal(key, (12, D), jnp.float32)
    row_pos = jnp.arange(12)[:, None]
    scales = jnp.where(row_pos < 6, 6.0 ** (-0.5), jnp.where(row_pos < 11, 0.3, D ** (-0.5)))
    return (values * scales).reshape(12 * D).astype(jnp.float32)


def with_ends(entries, own_key, least, high):
    longest = entries.shape.index(max(entries.shape))
    spots = []
    for shift in (0, 1):
        where = [jax.random.randint(jax.random.fold_in(own_key, axis), (), 0, length) for axis, length in enumerate(entries.shape)]
        where[longest] = (where[longest] + shift) % entries.shape[longest]
        spots.append(tuple(where))
    return entries.at[spots[0]].set(least).at[spots[1]].set(high)


def shard_levels(rng, shape, pieces, least, high):
    gain, own = 1.0, jax.random.fold_in(rng, 6)
    for axis_at, parts in pieces:
        draws = jnp.exp(jax.random.uniform(jax.random.fold_in(own, axis_at), (parts,), jnp.float32, least / len(pieces), high / len(pieces)))
        gain = gain * jnp.repeat(draws, shape[axis_at] // parts).reshape([-1 if axis == axis_at else 1 for axis in range(len(shape))])
    return gain


def centred(rng, dims, deviation, most, cuts=(), kind=jnp.bfloat16):
    values = jax.random.normal(rng, dims, jnp.float32) * deviation
    if len(cuts) > 0:
        values = shard_levels(rng, dims, cuts, -0.22, 0.18) * values
    return jnp.clip(values, min=-most, max=most).astype(kind)


def setup_inputs(seed: int = 0) -> dict:
    splits = jax.random.split(jax.random.key(seed), 12)
    return {
        "src_coords": jnp.clip(jax.random.uniform(splits[0], (3, NSRC), jnp.float32, -1.0, 1.0) * shard_levels(splits[0], (3, NSRC), ((1, 8),), -0.4, 0.0), -1.0, 1.0),
        "rcv_coords": jnp.clip(jax.random.uniform(splits[1], (3, NSRC, NRCV), jnp.float32, -1.0, 1.0) * shard_levels(splits[1], (3, NSRC, NRCV), ((1, 8), (2, 4)), -0.4, 0.0), -1.0, 1.0),
        "velocity": jnp.clip(jnp.exp(math.log(2.0) - 1.3862944 * jax.random.uniform(splits[2], (NSRC, NRCV), jnp.float32) ** shard_levels(splits[2], (NSRC, NRCV), ((0, 8), (1, 4)), -0.2, 0.2)), 0.5, 2.0),
        "pair_mask": draw_pair_mask(jax.random.fold_in(splits[11], 71), 0),
        "near_flag": with_ends((jax.random.randint(splits[4], (NSRC, NRCV), 0, 8) < 1).astype(jnp.int32), jax.random.fold_in(splits[4], 1), 0, 1),
        "block_params": centred(splits[5], (4 * D, D), D ** -0.5, 0.25, ((0, 32),), jnp.float32),
        "edge_params": draw_edge_params(jax.random.fold_in(splits[11], 71), 0),
        "block_moment": centred(splits[7], (4 * D, D), (0.05 / (4 * D * D + 12 * D) ** 0.5), 0.0007324219, ((0, 32),), jnp.float32),
        "edge_moment": centred(splits[8], (12 * D,), (0.15 / (4 * D * D + 12 * D) ** 0.5), 0.001953125, ((0, 32),), jnp.float32),
        "block_second": jnp.clip(jnp.exp(math.log(9.481189167104276e-09) - 1.3862944 * jax.random.uniform(splits[9], (4 * D, D), jnp.float32) ** shard_levels(splits[9], (4 * D, D), ((0, 32),), -0.2, 0.2)), 2.370297291776069e-09, 9.481189167104276e-09),
        "edge_second": jnp.clip(jnp.exp(math.log(8.533070428029532e-08) - 1.3862944 * jax.random.uniform(splits[10], (12 * D,), jnp.float32) ** shard_levels(splits[10], (12 * D,), ((0, 32),), -0.2, 0.2)), 2.133267607007383e-08, 8.533070428029532e-08),
    }


clip_limit = 0.05
beta_one = 0.5
beta_two = 0.5
adam_eps = 1e-08
decay_rate = 0.01
block_rate = 0.02
edge_rate = 0.1

@jax.custom_vjp
def low(v):
    return lax.optimization_barrier(v.astype(jnp.bfloat16)).astype(jnp.float32)

@jax.custom_vjp
def low_back(v):
    return v

def low_keep(v):
    return (low(v), None)

def low_pass(kept, grad):
    return (grad,)

def back_keep(v):
    return (v, None)

def back_low(kept, grad):
    return (low(grad),)
low.defvjp(low_keep, low_pass)
low_back.defvjp(back_keep, back_low)

def matmul(left, right):
    return jnp.dot(left, right, precision=lax.Precision.HIGHEST)

def elu_slope(values):
    return jnp.where(values > 0, 1.0, jnp.exp(jnp.minimum(values, 0.0)))

def pair_loss(block_params, edge_params, sources, points_raw, velocity, live_pair, near_pair):
    feat_width = block_params.shape[1]
    edge_table = edge_params.reshape(12, feat_width)
    points = jnp.where(near_pair[None] == 1, sources + 0.1 * points_raw, points_raw)
    inputs = jnp.concatenate([sources, points], 0)
    hidden = matmul(inputs.T, edge_table[:6]) + edge_table[6]
    pair_total = hidden.shape[0]
    tangent = jnp.broadcast_to(edge_table[3:6][:, None, :], (3, pair_total, feat_width))
    stream = jnp.concatenate([hidden[None], tangent], 0)
    for layer_idx in range(2):
        result = stream
        for half_idx in range(2):
            which = 2 * layer_idx + half_idx
            matrix = block_params[which * feat_width:(which + 1) * feat_width]
            mapped = matmul(result.reshape(-1, feat_width), matrix).reshape(4, pair_total, feat_width)
            preact = mapped[0] + edge_table[7 + which]
            result = jnp.concatenate([jax.nn.elu(preact)[None], elu_slope(preact)[None] * mapped[1:]], 0)
        stream = stream + result
    output = matmul(stream.reshape(-1, feat_width), edge_table[11]).reshape(4, pair_total)
    net_out = output[0]
    net_slope = output[1:]
    travel_ratio = jnp.sqrt(net_out * net_out + 1.0)
    ratio_slope = (net_out / travel_ratio)[None] * net_slope
    offset_vec = points - sources
    distance = jnp.sqrt(lax.optimization_barrier(jnp.sum(offset_vec * offset_vec, 0)) + 0.01)
    time_grad = travel_ratio[None] * offset_vec / distance[None] + distance[None] * ratio_slope
    grad_size = jnp.sqrt(lax.optimization_barrier(jnp.sum(time_grad * time_grad, 0)) + 0.01)
    misfit = velocity * grad_size - 1.0
    return jnp.sum(live_pair * misfit * misfit)

def adamw(weights, grads, first, second, rate):
    first_new = beta_one * first + (1.0 - beta_one) * grads
    second_new = beta_two * second + (1.0 - beta_two) * grads * grads
    first_hat = first_new / (1.0 - beta_one ** ADAM_STEP)
    second_hat = second_new / (1.0 - beta_two ** ADAM_STEP)
    weights_new = weights - rate * (first_hat / (jnp.sqrt(second_hat) + adam_eps) + decay_rate * weights)
    return (weights_new, first_new, second_new)

def reference(src_coords, rcv_coords, velocity, pair_mask, near_flag, block_params, edge_params, block_moment, edge_moment, block_second, edge_second):
    groups = NSRC // 4
    src_groups = src_coords.reshape(3, groups, 4).transpose(1, 0, 2)
    rcv_groups = rcv_coords.reshape(3, groups, 4, NRCV).transpose(1, 0, 2, 3)
    vel_groups = velocity.reshape(groups, 4, NRCV)
    live_all = pair_mask.astype(jnp.float32)
    live_groups = live_all.reshape(groups, 4, NRCV)
    near_groups = near_flag.reshape(groups, 4, NRCV)

    def group_terms(carry, packed):
        src_one, rcv_one, vel_one, live_one, near_one = packed
        sources = jnp.broadcast_to(src_one[:, :, None], rcv_one.shape).reshape(3, -1)

        def loss_part(bparams, eparams):
            return pair_loss(bparams, eparams, sources, rcv_one.reshape(3, -1), vel_one.reshape(-1), live_one.reshape(-1), near_one.reshape(-1))
        value_part, pullback = jax.vjp(loss_part, block_params, edge_params)
        grad_b, grad_e = pullback(jnp.float32(1.0))
        return ((carry[0] + grad_b, carry[1] + grad_e), value_part)
    start = (jnp.zeros_like(block_params), jnp.zeros_like(edge_params))
    (raw_b, raw_e), losses = lax.scan(group_terms, start, (src_groups, rcv_groups, vel_groups, live_groups, near_groups))
    count_all = jnp.maximum(jnp.sum(live_all), 1.0)
    total_sq = jnp.sum(raw_b * raw_b) + jnp.sum(raw_e * raw_e)
    grad_norm = jnp.sqrt(total_sq) / count_all
    clip_factor = jnp.minimum(1.0, clip_limit / (grad_norm + 1e-06))
    grads_b = raw_b * clip_factor / count_all
    grads_e = raw_e * clip_factor / count_all
    new_blocks, moment_blocks, second_blocks = adamw(block_params, grads_b, block_moment, block_second, block_rate)
    new_edges, moment_edges, second_edges = adamw(edge_params, grads_e, edge_moment, edge_second, edge_rate)
    return (grad_norm, new_blocks, new_edges, moment_blocks, moment_edges, second_blocks, second_edges, new_blocks.astype(jnp.bfloat16), new_edges.astype(jnp.bfloat16))
```

```python
import functools

import jax
import jax.numpy as jnp
from jax import lax
from jax.experimental import pallas as pl
from jax.experimental.pallas import tpu as pltpu
from jax.sharding import PartitionSpec as P

ADAM_STEP = 5
D = 512
CHUNK = 256
TILE = 64

clip_limit = 0.05
beta_one = 0.5
beta_two = 0.5
adam_eps = 1e-08
decay_rate = 0.01
block_rate = 0.02
edge_rate = 0.1

F32 = jnp.float32
BF16 = jnp.bfloat16
F8 = jnp.float8_e4m3fn
SMALL = pltpu.CompilerParams(vmem_limit_bytes=8 * 1024 * 1024)
NN = (((1,), (0,)), ((), ()))
NT = (((1,), (1,)), ((), ()))
AXES = ("k", "b", "x", "c")
FACTORS = 8 * D // 128


def dot(left, right, dims=NN):
    return lax.dot_general(left, right, dims, preferred_element_type=F32)


def split(x):
    high = x.astype(BF16)
    return high, (x - high.astype(F32)).astype(BF16)


def scale_of(bound):
    return 256.0 / jnp.maximum(bound, 1e-30)


def parts(x, scale):
    high = x.astype(BF16)
    left = (x - high.astype(F32)).astype(BF16)
    whole, left = high * scale.astype(BF16), left * (scale * 256.0).astype(BF16)
    return high, whole.astype(F8), left.astype(F8)


def largest(x):
    return jnp.max(jnp.abs(x), (0, 1), keepdims=True)


def tiles(stage, *arrays):
    cuts = [slice(at, at + TILE) for at in range(0, D, TILE)]
    done = [stage(*(one(cut) if callable(one) else one[cut] for one in arrays)) for cut in cuts]
    return tuple(jnp.concatenate(one, 0) for one in zip(*done))


def stack(x):
    return x.reshape(-1, 8, x.shape[1])


def top_of(x):
    return jnp.max(stack(jnp.abs(x)), 0)


def sum_of(x):
    return jnp.sum(stack(x), 0)


def weigh(weights, k, x):
    main, small, scales = weights
    high, whole, left, scale = x
    rest = dot(small[k], jnp.concatenate([left, whole], 0))
    return dot(main[k], high) + rest * (scales[k : k + 1, 0:1] / (256.0 * scale))


def outer(*terms):
    lefts, rights = ([one for term in terms for one in term[side]] for side in range(2))
    main = [jnp.concatenate([one[0] for one in side], 1) for side in (lefts, rights)]
    total = dot(*main, NT)
    for lefts, rights in terms:
        wide = jnp.concatenate([part for one in lefts for part in one[1:3]], 1)
        back = jnp.concatenate([part for one in rights for part in (one[2], one[1])], 1)
        total = total + dot(wide, back, NT) * (1.0 / (256.0 * lefts[0][3] * rights[0][3]))
    return total


def elu_parts(c):
    above = c > 0
    slope = jnp.exp(jnp.minimum(c, 0.0))
    curve = jnp.where(above, 0.0, jnp.where(c < 0, slope, 0.5))
    return jnp.where(above, c, slope - 1.0), slope, curve


def fold(x):
    total = x[:, :128]
    for at in range(128, x.shape[1], 128):
        total = total + x[:, at : at + 128]
    return total


def pair_kernel(layout, lanes, src_ref, rcv_ref, vel_ref, live_ref, near_ref, *refs):
    shared_edges = lanes != 4
    if shared_edges:
        e_ref, refs = refs[0], refs[1:]
    pieces, refs = refs[: len(layout)], refs[len(layout) :]
    aways, keeps, refs = refs[:lanes], refs[lanes : 2 * lanes], refs[2 * lanes :]
    small_ref, table_ref, dw_ref, full, left, et, limits, sums, wide, sems = refs[:10]
    wn, wt = refs[10:13], refs[13:16]
    rows = D // (2 * lanes)
    which, core = lax.axis_index("k"), lax.axis_index("c")
    lane = lax.axis_index(("b", "x"))

    shard = rows // 2 + (0 if shared_edges else 1)

    def matrix(k):
        lines = []
        for place in range(2 * lanes):
            first = (2 * lanes * k + place) * shard
            columns = [full[pl.ds(first + at, rows // 8, D // 128)] for at in range(D // 128)]
            lines.append(jnp.concatenate([one.reshape(rows, 128) for one in columns], 1))
        return jnp.concatenate(lines, 0)

    def edge_table():
        lines = []
        for at in range(4 * lanes):
            even, odd = (full[(2 * at + one) * shard + shard - 1] for one in range(2))
            lines += [even[0:1], even[1:2] + odd[0:1], odd[1:2]]
        wide_lines = [jnp.concatenate(lines[4 * at : 4 * at + 4], 1) for at in range(12)]
        return jnp.concatenate(wide_lines + [jnp.zeros((4, D), F32)], 0)

    def start(copies):
        copies = [pltpu.make_async_copy(a, b, sems.at[at]) for at, (a, b) in enumerate(copies)]
        for one in copies:
            one.start()
        return copies

    copies = []
    for ref, segments in zip(pieces, layout):
        for plane, other, swapped, at, first, size in segments:
            place = (lane ^ other) * 2 + (core ^ swapped)
            to = ((which ^ plane) * 2 * lanes + place) * shard + first
            to = full.at[pl.ds(to, size)]
            copies.append((ref.at[pl.ds(at, size)], to))
    for one in start(copies):
        one.wait()
    for k in range(3):
        plain = matrix(k + 1)
        for (main, small, scales), one in ((wn, plain), (wt, plain.T)):
            scale = scale_of(largest(one))
            main[k], small[k, :, :D], small[k, :, D:] = parts(one, scale)
            scales[k : k + 1] = jnp.broadcast_to(1.0 / scale, (1, 128))
            reach = jnp.max(jnp.sum(jnp.abs(one.T if main is wn[0] else plain), 0, keepdims=True))
            scales[4 + k : 5 + k] = jnp.full((1, 128), reach, F32)
    edge = e_ref[...] if shared_edges else edge_table()
    table_ref[...] = edge
    row = lax.broadcasted_iota(jnp.int32, (8, D), 0)
    first = jnp.where(row < 7, edge[:8], 0.0)
    fh, fl = split(first)
    wh, wl = split(matrix(0))
    mixed = dot(fh, wh) + dot(fh, wl) + dot(fl, wh)
    biased = mixed + jnp.where(row == 6, edge[7:8], 0.0)
    columns = jnp.concatenate([edge[8:12], edge[3:6], mixed[3:6], jnp.zeros((118, D), F32)], 0).T
    for at in range(10):
        et[at] = jnp.broadcast_to(columns[:, at : at + 1], (D, 128))
    rows_of = [edge[:8], biased, edge[8:16], mixed]
    for at, part in enumerate(rows_of):
        limits[8 * at : 8 * at + 8] = jnp.broadcast_to(
            jnp.max(jnp.abs(part), 1, keepdims=True), (8, 128)
        )
    tang = jnp.where(row < 3, pltpu.roll(first, 5, 0), 0.0)
    tang_mixed = jnp.where(row < 3, pltpu.roll(mixed, 5, 0), 0.0)
    for at, part in enumerate((first, biased, tang, tang_mixed)):
        high, low = split(part)
        cat = jnp.concatenate(
            [high.astype(F32), high.astype(F32), low.astype(F32), jnp.zeros((104, D), F32)], 0
        ).T
        left[at] = cat.astype(BF16)

    def column(at):
        return lambda cut: jnp.concatenate([et[at, cut]] * (CHUNK // 128), 1)

    chunks = range(rcv_ref.shape[2] // CHUNK)
    blocks = [(at, one) for at in range(src_ref.shape[0]) for one in chunks]

    def each(stage, *lists):
        return [stage(*one) for one in zip(*lists)]

    def both(stage, *lists):
        return tuple(zip(*each(stage, *lists)))

    def triple(x):
        high, low = (part.astype(F32) for part in split(x))
        return jnp.concatenate([high, low, high, jnp.zeros((104, CHUNK), F32)], 0).astype(BF16)

    def points(step, b):
        lanes_of = slice(b * CHUNK, (b + 1) * CHUNK)
        near = near_ref[pl.ds(step, 1), lanes_of] == 1
        source = src_ref[step]
        p = [jnp.concatenate([source[j : j + 1]] * (CHUNK // 128), 1) for j in range(3)]
        raw = [rcv_ref[j, pl.ds(step, 1), lanes_of] for j in range(3)]
        q = [jnp.where(near, a + 0.1 * b, b) for a, b in zip(p, raw)]
        ends = [jnp.ones((1, CHUNK), F32), jnp.zeros((1, CHUNK), F32)]
        return jnp.concatenate(p + q + ends, 0)

    x = [points(*one) for one in blocks]
    vel = [vel_ref[pl.ds(at, 1), b * CHUNK : (b + 1) * CHUNK] for at, b in blocks]
    live = [live_ref[pl.ds(at, 1), b * CHUNK : (b + 1) * CHUNK].astype(F32) for at, b in blocks]
    x_wide = each(triple, x)
    h0 = each(lambda one: dot(left[0], one), x_wide)
    a0 = each(lambda one: dot(left[1], one), x_wide)

    def reach(weights, k, x):
        return weights[2][4 + k : 5 + k, 0:1] * x

    def limit(at):
        return limits[at : at + 1, 0:1]

    def over_rows(first, count, x):
        sizes = jnp.max(jnp.abs(x[:count]), 1, keepdims=True)
        return jnp.sum(limits[first : first + count, 0:1] * sizes, 0, keepdims=True)

    def graded(stage, bounds, *lists):
        def run(scale, *arrays):
            def one(*cut):
                x, *rest = stage(*cut)
                high, whole, left = parts(x, scale)
                top = jnp.max(jnp.abs(high).reshape(-1, 16, CHUNK), 0).astype(F32)
                return (high, whole, left, top, *rest)

            high, whole, left, top, *rest = tiles(one, *arrays)
            return (high, whole, left, scale), largest(top), *rest

        scale = scale_of(functools.reduce(jnp.maximum, bounds))
        return both(run, again(scale), *lists)

    def again(one):
        return [one] * len(blocks)

    def enter(c, bias):
        return elu_parts(c + bias)

    def add_half(c, bias, h):
        v, s, k = elu_parts(c + bias)
        return h + v, s, k

    u0s, top, s0, k0 = graded(elu_parts, each(lambda x: over_rows(8, 7, x), x), a0)
    c1 = each(lambda one: weigh(wt, 0, one), u0s)
    bounds = each(lambda x, top: over_rows(0, 7, x) + reach(wt, 0, top) + limit(16), x, top)
    h1s, top, s1, k1, h1 = graded(
        lambda *one: (lambda h, s, k: (h, s, k, h))(*add_half(*one)), bounds, c1, again(column(0)), h0
    )
    a2 = each(lambda one: weigh(wt, 1, one), h1s)
    bounds = each(lambda top: reach(wt, 1, top) + limit(17), top)
    u2s, _, s2, k2 = graded(enter, bounds, a2, again(column(1)))
    c3 = each(lambda one: weigh(wt, 2, one), u2s)

    def last_half(c, bias, h, e):
        h, s, k = add_half(c, bias, h)
        return s * e, h, s, k, sum_of(h * e)

    e_top = limit(19)
    y3, top, h2, s3, k3, out = graded(last_half, again(e_top), c3, again(column(2)), h1, again(column(3)))
    out = each(lambda one: jnp.sum(one, 0, keepdims=True), out)

    l2 = each(lambda one: weigh(wn, 2, one), y3)
    bounds = each(lambda top: reach(wn, 2, top), top)
    y2, top, q2 = graded(lambda l, s, k: (s * l, l * k), bounds, l2, s2, k2)
    l1 = each(lambda one: weigh(wn, 1, one), y2)
    bounds = each(lambda top: reach(wn, 1, top) + e_top, top)

    def back_add(value, e, s, k):
        value = value + e
        return s * value, value, value * k

    y1, _, lh1, q1 = graded(back_add, bounds, l1, again(column(3)), s1, k1)
    l0 = each(lambda one: weigh(wn, 0, one), y1)

    def leave(value, s, k, h, *columns):
        y = s * value
        sums = [sum_of(h * columns[j] + y * columns[3 + j]) for j in range(3)]
        return y, value * k, *sums

    y0, q0, *slope = both(
        lambda *one: tiles(leave, *one, *(column(4 + j) for j in range(6))), l0, s0, k0, lh1
    )
    slope = each(
        lambda *one: jnp.concatenate([jnp.sum(part, 0, keepdims=True) for part in one], 0), *slope
    )

    def loss_slopes(x, vel, live, out, slope):
        p, q = x[0:3], x[3:6]
        ratio = jnp.sqrt(out * out + 1.0)
        part = out / ratio
        off = q - p
        dist = jnp.sqrt(jnp.sum(off * off, 0, keepdims=True) + 0.01)
        unit = off / dist
        grad = ratio * unit + dist * part * slope
        size = jnp.sqrt(jnp.sum(grad * grad, 0, keepdims=True) + 0.01)
        misfit = vel * size - 1.0
        d_grad = (2.0 * live * misfit * vel / size) * grad
        d_slope = d_grad * (dist * part)
        d_ratio = jnp.sum(d_grad * unit, 0, keepdims=True)
        d_part = jnp.sum(d_grad * slope, 0, keepdims=True) * dist
        inv = 1.0 / ratio
        d_out = d_ratio * part + d_part * (inv * inv * inv)
        return d_out, jnp.concatenate([d_slope, jnp.zeros((5, CHUNK), F32)], 0)

    d_out, om = both(loss_slopes, x, vel, live, out, slope)
    om_wide = each(triple, om)
    t0 = each(lambda one: dot(left[2], one), om_wide)
    m0 = each(lambda one: dot(left[3], one), om_wide)

    bounds = each(lambda om: over_rows(27, 3, om), om)
    du0, top, q0 = graded(lambda m, s, q: (s * m, m * q), bounds, m0, s0, q0)
    n1 = each(lambda one: weigh(wt, 0, one), du0)
    bounds = each(lambda om, top: over_rows(3, 3, om) + reach(wt, 0, top), om, top)

    def along_add(n, t, s, q):
        t = t + s * n
        q = n * q
        return t, t, q, top_of(q)

    t1s, top, t1, q1, q1_top = graded(along_add, bounds, n1, t0, s1, q1)
    m2 = each(lambda one: weigh(wt, 1, one), t1s)

    def along(m, s, q):
        q = m * q
        return s * m, q, top_of(q)

    bounds = each(lambda top: reach(wt, 1, top), top)
    du2, top, q2, q2_top = graded(along, bounds, m2, s2, q2)
    n3 = each(lambda one: weigh(wt, 2, one), du2)

    def turn(n, s, k, t, h, e, d):
        cb = e * (d * s + n * k)
        return cb, fold(cb), fold(d * h + t + s * n)

    def down(u, s, q):
        ab = u * s + q
        return ab, fold(ab)

    def down_add(u, e, s, q, lh, d, x, om):
        hb = u + d * e
        cb = hb * s + q
        return cb, fold(cb), fold(hb), *weighted(hb, lh, x, om)

    def end(u, s, q, y, x, om):
        ab = u * s + q
        return fold(ab), *weighted(ab, y, x, om)

    def weighted(value, other, x, om):
        return [fold(value * x[3 + j : 4 + j] + other * om[j : j + 1]) for j in range(3)]

    def same(one):
        return lambda cut: one

    d_top = each(largest, d_out)
    d_all, x_all, om_all = (each(same, one) for one in (d_out, x, om))
    bounds = each(lambda d, top: e_top * (d + reach(wt, 2, top)), d_top, top)
    cb3, top, *sum3 = graded(turn, bounds, n3, s3, k3, t1, h2, again(column(3)), d_all)
    ub2 = each(lambda one: weigh(wn, 2, one), cb3)
    dw_ref[2] = outer((u2s, cb3), (du2, y3))
    bounds = each(lambda top, q: reach(wn, 2, top) + largest(q), top, q2_top)
    ab2, top, *sum2 = graded(down, bounds, ub2, s2, q2)
    hb1 = each(lambda one: weigh(wn, 1, one), ab2)
    dw_ref[1] = outer((h1s, ab2), (t1s, y2))
    bounds = each(lambda d, top, q: e_top * d + reach(wn, 1, top) + largest(q), d_top, top, q1_top)
    cb1, _, *sum1 = graded(down_add, bounds, hb1, again(column(3)), s1, q1, lh1, d_all, x_all, om_all)
    ub0 = each(lambda one: weigh(wn, 0, one), cb1)
    dw_ref[0] = outer((u0s, cb1), (du0, y1))
    sum0 = both(
        lambda u, s, q, y, a, b: tiles(end, u, s, q, y, same(a), same(b)), ub0, s0, q0, y0, x, om
    )
    for at, terms in enumerate((sum1[0], sum2[0], sum3[0], sum3[1])):
        sums[at] = sum(terms)
    for at, (ones, *points_of) in enumerate((sum0, sum1[1:])):
        wide[at, 6] = sum(ones)
        for j in range(3):
            wide[at, j] = sum(src_ref[one, j : j + 1] * part for (one, _), part in zip(blocks, ones))
            wide[at, 3 + j] = sum(points_of[j])

    copies = []
    for half, refs in ((1 - core, aways), (core, keeps)):
        for other in reversed(range(lanes)):
            first = pl.multiple_of((2 * (lane ^ other) + half) * rows, 8)
            for k in range(3):
                there = refs[other].at[pl.ds(k * rows, rows)]
                copies.append((dw_ref.at[k, pl.ds(first, rows)], there))
    copies = start(copies)

    row = lax.broadcasted_iota(jnp.int32, (8, D), 0)

    def gather(at):
        lines = [jnp.sum(wide[at, one].T, 0, keepdims=True) for one in range(7)]
        return jnp.concatenate(lines + [jnp.zeros((1, D), F32)], 0)

    g, h = gather(0), gather(1)
    gh_, gl_ = split(g)
    wh, wl = split(matrix(0))
    first = h + dot(gh_, wh, NT) + dot(gh_, wl, NT) + dot(gl_, wh, NT)
    first = jnp.where(row < 7, first, g[6:7])
    tails = [jnp.sum(sums[at].T, 0, keepdims=True) for at in range(4)]
    small_ref[0:8] = first
    small_ref[8:16] = jnp.concatenate(tails + [jnp.zeros((4, D), F32)], 0)
    small_ref[16:24] = jnp.where(row < 7, g, 0.0)
    for one in copies:
        one.wait()


def pair_grads(pairs, edges, pieces, layout, lanes):
    rows = D // (2 * lanes)
    sent = [jax.ShapeDtypeStruct((3 * rows, D), F32)] * (2 * lanes)
    count = pairs[1].shape[1] * pairs[1].shape[2]
    segments = sum(len(one) for one in layout)
    vmem, held = pl.BlockSpec(memory_space=pltpu.VMEM), pl.BlockSpec(memory_space=pl.ANY)
    outs = pl.pallas_call(
        functools.partial(pair_kernel, layout, lanes),
        in_specs=[vmem] * (5 + len(edges)) + [held] * len(pieces),
        out_specs=[held] * len(sent) + [vmem] * 2,
        out_shape=sent
        + [jax.ShapeDtypeStruct((24, D), F32), jax.ShapeDtypeStruct((16, D), F32)],
        scratch_shapes=[
            pltpu.VMEM((3, D, D), F32),
            pltpu.VMEM((8 * lanes * (rows // 2 + (lanes == 4)), 8, 128), F32),
            pltpu.VMEM((4, D, 128), BF16),
            pltpu.VMEM((10, D, 128), F32),
            pltpu.VMEM((32, 128), F32),
            pltpu.VMEM((4, D, 128), F32),
            pltpu.VMEM((2, 7, D, 128), F32),
            pltpu.SemaphoreType.DMA((max(segments, 6 * lanes),)),
        ]
        + [
            pltpu.VMEM((3, D, D), BF16),
            pltpu.VMEM((3, D, 2 * D), F8),
            pltpu.VMEM((8, 128), F32),
        ]
        * 2,
        compiler_params=pltpu.CompilerParams(vmem_limit_bytes=60 * 1024 * 1024),
        cost_estimate=pl.CostEstimate(
            flops=54 * 2 * count * D * D, bytes_accessed=8 * 1024 * 1024, transcendentals=4 * count * D
        ),
    )(*pairs, *edges, *pieces)
    return outs[:lanes], outs[lanes : 2 * lanes], *outs[2 * lanes :]


def adamw(weights, grads, first, second, rate):
    first_new = beta_one * first + (1.0 - beta_one) * grads
    second_new = beta_two * second + (1.0 - beta_two) * grads * grads
    first_hat = first_new / (1.0 - beta_one**ADAM_STEP)
    second_hat = second_new / (1.0 - beta_two**ADAM_STEP)
    weights_new = weights - rate * (
        first_hat / (jnp.sqrt(second_hat) + adam_eps) + decay_rate * weights
    )
    return (weights_new, first_new, second_new)


def exchange(x, plane, other, swapped, lanes):
    total = 8 * lanes
    mask = (plane * lanes + other) * 2 + swapped
    return lax.ppermute(x, AXES, [(i, i ^ mask) for i in range(total)])


def in_turn(first, *others):
    done = (first,)
    for one in others:
        one, *done = lax.optimization_barrier((one, *done))
        done = (*done, one)
    return done


def as_tiles(own):
    rows = own.shape[0]
    tiled = own.reshape(rows // 8, 8, D // 128, 128).transpose(0, 2, 1, 3)
    return tiled.reshape(rows // 2, 8, 128)


def spread(own, edges, sources, lanes):
    size = own.shape[0] // 2 + (lanes == 4)
    own = as_tiles(own)

    def at(plane, other, first=0):
        return [(plane, other, 0, first, 0, size)]

    def to_core(array):
        return exchange(array, 0, 0, 1, lanes)

    def to_place(array, other):
        return exchange(array, 0, other, 0, lanes)

    if lanes != 4:
        far = [exchange(own, plane, 0, 0, lanes) for plane in (1, 2, 3)]
        stack = jnp.concatenate([own] + far, 0)
        got = [
            (to_place(stack, other) if other else stack, sum((at(p, other, p * size) for p in range(4)), []))
            for other in range(lanes)
        ]
        swaps = [to_core(array) for array, _ in got]
    else:
        odd = lax.axis_index("c") == 1
        line = jnp.where(odd, jnp.pad(edges, (64, 0)), jnp.pad(edges, (0, 64)))
        line = jnp.pad(line.reshape(1, 2, 128), ((0, 0), (0, 6), (0, 0)))
        own = jnp.concatenate([own, line], 0)
        far = [exchange(own, plane, 0, 0, lanes) for plane in (1, 2, 3)]
        near = [to_place(own, other) for other in (1, 2)]
        diagonal = to_place(own, 3)
        far[0], sources, far[1], far[2], near[1], near[0], diagonal = in_turn(
            far[0], sources, far[1], far[2], near[1], near[0], diagonal
        )
        early = [own, *near, diagonal]
        stack = jnp.concatenate(far, 0)
        more = [to_place(stack, other) for other in (1, 2)]
        swaps = [to_core(array) for array in early[:3]]
        ahead = more[1]
        more[1], more[0], *swaps = in_turn(more[1], more[0], *swaps)
        half = 3 * size // 2
        ends = [to_place(ahead[:half], 1), to_place(more[0][half:], 2)]
        swaps += [to_core(array) for array in (diagonal, stack, *more)]
        tied = in_turn(*ends, *swaps)
        ends, swaps = tied[:2], list(tied[2:])

        def three(other):
            return sum((at(p, other, (p - 1) * size) for p in (1, 2, 3)), [])

        def cut(segments, low, high):
            found = []
            for plane, other, core, here, first, count in segments:
                start, stop = max(here, low), min(here + count, high)
                if start < stop:
                    found.append((plane, other, core, start - low, first + start - here, stop - start))
            return found

        got = [(array, at(0, other)) for other, array in enumerate(early)]
        got += [(stack, three(0)), (more[0], three(1)), (more[1], three(2))]
        got += [(ends[0], cut(three(3), 0, half)), (ends[1], cut(three(3), half, 3 * size))]
        swaps += [to_core(array) for array in ends]
    got += [
        (array, [(a, b, 1, *rest) for a, b, _, *rest in segments])
        for array, (_, segments) in zip(swaps, list(got))
    ]
    return [array for array, _ in got], [tuple(segments) for _, segments in got], sources


def local(
    lanes,
    src_coords,
    rcv_coords,
    velocity,
    pair_mask,
    near_flag,
    block_params,
    edge_params,
    block_moment,
    edge_moment,
    block_second,
    edge_second,
):
    plane = 2 * lanes
    total = 4 * plane
    rows = block_params.shape[0]
    which, core = lax.axis_index("k"), lax.axis_index("c")
    me = lax.axis_index(AXES)

    def to_all(x):
        return lax.all_to_all(x, AXES, 0, 0, tiled=True)

    share = edge_params.shape[0]
    sources = jnp.broadcast_to(src_coords.T.reshape(-1, 3, 1), (src_coords.shape[1], 3, 128))
    edges = []
    if lanes != 4:
        edges = to_all(jnp.broadcast_to(edge_params[None, None], (total, 1, share)))
        edges = [jnp.pad(edges.reshape(12, D), ((0, 4), (0, 0)))]
    pieces, layout, sources = spread(block_params, edge_params, sources, lanes)
    pairs = (sources, rcv_coords, velocity, pair_mask, near_flag)
    away, keep, small, edges = pair_grads(pairs, edges, pieces, layout, lanes)

    arrived = []
    for other in reversed(range(lanes)):
        part = keep[other] + exchange(away[other], 0, 0, 1, lanes)
        arrived.append(exchange(part, 0, other, 0, lanes) if other else part)
    arrived = [*in_turn(*arrived[:-1]), arrived[-1]]
    shares = [small[:12].reshape(total, 1, share), small[16:24].reshape(FACTORS, 1, -1)]
    shares[1] = jnp.pad(shares[1], ((0, total - FACTORS), (0, 0), (0, 0)))
    shares = to_all(jnp.concatenate(shares, 2))

    arrived[0], shares = lax.optimization_barrier((arrived[0], shares))

    def rows_of(matrix):
        at = jnp.maximum(matrix - 1, 0) * rows
        return sum(lax.dynamic_slice_in_dim(one, at, rows, 0) for one in arrived)

    owned = []
    for other in (3, 2, 1):
        perm = [(i, i ^ (other * plane)) for i in range(total)]
        owned.append(lax.ppermute(rows_of(which ^ other), AXES, perm))
    owned = [*in_turn(*owned), rows_of(which)]

    kind = which.astype(jnp.int32).reshape(1)
    owned, own_edges, shared = collect(kind, owned, shares, pair_mask, share)
    shared = to_all(shared)
    own_first = lax.dynamic_slice_in_dim(edges[:8], me % plane * rows, rows, 1).T
    return update(
        kind,
        (shared, edges[:8], own_first),
        (owned, block_params, block_moment, block_second),
        (own_edges, edge_params, edge_moment, edge_second),
    )


def collect_kernel(kind_ref, shares_ref, mask_ref, *refs):
    owned_ref, edges_ref, shared_ref = refs[-3:]
    share = edges_ref.shape[1]
    kind = kind_ref[0]

    owned_ref[...] = jnp.where(kind == 0, 0.0, sum(one[...] for one in refs[:-3]))
    shares = jnp.sum(shares_ref[...], 0)
    own = shares[:, :share]
    edges_ref[...] = own

    def whole(x):
        return jnp.sum(jnp.sum(x, 0, keepdims=True), 1, keepdims=True)

    squares = whole(owned_ref[...] * owned_ref[...]) + whole(own * own)
    live = whole(mask_ref[...].astype(F32))
    lane = lax.broadcasted_iota(jnp.int32, (1, 128), 1)
    sums = jnp.where(lane == 0, squares, jnp.where(lane == 1, live, 0.0))
    line = jnp.concatenate([sums, shares[:, share:]], 1)
    shared_ref[...] = jnp.broadcast_to(line[None], shared_ref.shape)


def collect(kind, owned, shares, mask, share):
    rows, total = owned[0].shape[0], shares.shape[0]
    smem, vmem = pl.BlockSpec(memory_space=pltpu.SMEM), pl.BlockSpec(memory_space=pltpu.VMEM)
    shapes = [(rows, D), (1, share), (total, 1, 256)]
    return pl.pallas_call(
        collect_kernel,
        in_specs=[smem] + [vmem] * (2 + len(owned)),
        out_specs=[vmem] * 3,
        out_shape=[jax.ShapeDtypeStruct(one, F32) for one in shapes],
        compiler_params=SMALL,
    )(kind, shares, mask, *owned)


def update_kernel(kind_ref, shared_ref, edge_ref, own_ref, *refs):
    ins, outs = refs[:8], refs[8:]
    shared = jnp.sum(shared_ref[:, :, :128], 0)
    lane = lax.broadcasted_iota(jnp.int32, shared.shape, 1)
    per = D // 128
    lines = [
        jnp.concatenate([shared_ref[at * per + one, :, 128:] for one in range(per)], 1)
        for at in range(8)
    ]
    factor, rows, own = jnp.concatenate(lines, 0), edge_ref[...], own_ref[...]
    first = jnp.zeros(ins[0].shape, F32)
    mixed = jnp.zeros_like(factor)
    for at in range(7):
        first = first + own[:, at : at + 1] * factor[at : at + 1]
        gram = jnp.sum(rows * rows[at : at + 1], 1, keepdims=True)
        mixed = mixed + gram * factor[at : at + 1]
    valid = lax.broadcasted_iota(jnp.int32, factor.shape, 0) < 7
    first_sq = jnp.sum(jnp.where(valid, mixed * factor, 0.0), 0, keepdims=True)
    first_sq = jnp.sum(first_sq, 1, keepdims=True)
    total_sq = jnp.sum(jnp.where(lane == 0, shared, 0.0), 1, keepdims=True) + first_sq
    count = jnp.sum(jnp.where(lane == 1, shared, 0.0), 1, keepdims=True)
    count = jnp.maximum(count, 1.0)
    grad_norm = jnp.sqrt(total_sq) / count
    outs[0][0] = grad_norm[0, 0]
    scale = jnp.minimum(1.0, clip_limit / (grad_norm + 1e-06)) / count
    for at, rate in ((0, block_rate), (4, edge_rate)):
        raw, weights, one, two = (ref[...] for ref in ins[at : at + 4])
        if at == 0:
            raw = jnp.where(kind_ref[0] == 0, first, raw)
        weights, one, two = adamw(weights, raw * scale, one, two, rate)
        outs[1 + at][...] = weights
        outs[2 + at][...] = one
        outs[3 + at][...] = two
        low = weights.astype(BF16)
        outs[4 + at][...] = low.reshape(outs[4 + at].shape)


def update(kind, shared, blocks, edges):
    edges = (edges[0],) + tuple(one[None] for one in edges[1:])
    smem, vmem = pl.BlockSpec(memory_space=pltpu.SMEM), pl.BlockSpec(memory_space=pltpu.VMEM)
    shapes = [(1,)] + [blocks[0].shape] * 4 + [edges[0].shape] * 3 + [edges[0].shape[1:]]
    types = [F32] + [F32, F32, F32, BF16] * 2
    outs = pl.pallas_call(
        update_kernel,
        in_specs=[smem] + [vmem] * 11,
        out_specs=[smem] + [vmem] * 8,
        out_shape=[jax.ShapeDtypeStruct(a, b) for a, b in zip(shapes, types)],
        compiler_params=SMALL,
    )(kind, *shared, *blocks, *edges)
    norm, new_b, moment_b, second_b, low_b, new_e, moment_e, second_e, low_e = outs
    new_e, moment_e, second_e = (one[0] for one in (new_e, moment_e, second_e))
    return norm.reshape(()), new_b, new_e, moment_b, moment_e, second_b, second_e, low_b, low_e


def solution(mesh):
    count_src, count_rcv = mesh.shape["src"], mesh.shape["rcv"]
    shape = (4, count_src // 4, count_rcv // 2, 2)
    split_mesh = jax.sharding.Mesh(mesh.devices.reshape(shape), AXES)
    src, rcv = ("k", "b"), ("x", "c")
    wide, flat = P(AXES, None), P(AXES)
    placed = (
        P(None, src),
        P(None, src, rcv),
        P(src, rcv),
        P(src, rcv),
        P(src, rcv),
        wide,
        flat,
        wide,
        flat,
        wide,
        flat,
    )
    return jax.shard_map(
        functools.partial(local, shape[1] * shape[2]),
        mesh=split_mesh,
        in_specs=placed,
        out_specs=(P(), wide, flat, wide, flat, wide, flat, wide, flat),
        check_vma=False,
    )
```

```python
import functools

import jax
import jax.numpy as jnp
from jax import lax
from jax.experimental import pallas as pl
from jax.experimental.pallas import tpu as pltpu
from jax.sharding import PartitionSpec as P

ADAM_STEP = 5
D = 512
CHUNK = 256
TILE = 64

clip_limit = 0.05
beta_one = 0.5
beta_two = 0.5
adam_eps = 1e-08
decay_rate = 0.01
block_rate = 0.02
edge_rate = 0.1

F32 = jnp.float32
BF16 = jnp.bfloat16
F8 = jnp.float8_e4m3fn
SMALL = pltpu.CompilerParams(vmem_limit_bytes=8 * 1024 * 1024)
NN = (((1,), (0,)), ((), ()))
NT = (((1,), (1,)), ((), ()))
AXES = ("k", "b", "x", "c")
PARTS = lambda lanes: 2 if lanes == 4 else 1
FACTORS = 8 * D // 128


def dot(left, right, dims=NN):
    return lax.dot_general(left, right, dims, preferred_element_type=F32)


def split(x):
    high = x.astype(BF16)
    return high, (x - high.astype(F32)).astype(BF16)


def scale_of(bound):
    return 256.0 / jnp.maximum(bound, 1e-30)


def parts(x, scale):
    high = x.astype(BF16)
    left = (x - high.astype(F32)).astype(BF16)
    whole, left = high * scale.astype(BF16), left * (scale * 256.0).astype(BF16)
    return high, whole.astype(F8), left.astype(F8)


def largest(x):
    return jnp.max(jnp.abs(x), (0, 1), keepdims=True)


def tiles(stage, *arrays):
    cuts = [slice(at, at + TILE) for at in range(0, D, TILE)]
    done = [stage(*(one(cut) if callable(one) else one[cut] for one in arrays)) for cut in cuts]
    return tuple(jnp.concatenate(one, 0) for one in zip(*done))


def stack(x):
    return x.reshape(-1, 8, x.shape[1])


def top_of(x):
    return jnp.max(stack(jnp.abs(x)), 0)


def sum_of(x):
    return jnp.sum(stack(x), 0)


def weigh(weights, k, x):
    main, small, scales = weights
    high, whole, left, scale = x
    rest = dot(small[k], jnp.concatenate([left, whole], 0))
    return dot(main[k], high) + rest * (scales[k : k + 1, 0:1] / (256.0 * scale))


def outer(*terms):
    lefts, rights = ([one for term in terms for one in term[side]] for side in range(2))
    main = [jnp.concatenate([one[0] for one in side], 1) for side in (lefts, rights)]
    total = dot(*main, NT)
    for lefts, rights in terms:
        wide = jnp.concatenate([part for one in lefts for part in one[1:3]], 1)
        back = jnp.concatenate([part for one in rights for part in (one[2], one[1])], 1)
        total = total + dot(wide, back, NT) * (1.0 / (256.0 * lefts[0][3] * rights[0][3]))
    return total


def elu_parts(c):
    above = c > 0
    slope = jnp.exp(jnp.minimum(c, 0.0))
    curve = jnp.where(above, 0.0, jnp.where(c < 0, slope, 0.5))
    return jnp.where(above, c, slope - 1.0), slope, curve


def fold(x):
    total = x[:, :128]
    for at in range(128, x.shape[1], 128):
        total = total + x[:, at : at + 128]
    return total


def pair_kernel(layout, lanes, src_ref, rcv_ref, vel_ref, live_ref, near_ref, *refs):
    shared_edges = lanes != 4
    if shared_edges:
        e_ref, refs = refs[0], refs[1:]
    pieces, refs = refs[: len(layout)], refs[len(layout) :]
    slots = lanes * PARTS(lanes)
    aways, keeps, refs = refs[:slots], refs[slots : 2 * slots], refs[2 * slots :]
    small_ref, table_ref, dw_ref, full, left, et, limits, sums, wide, sems = refs[:10]
    wn, wt = refs[10:13], refs[13:16]
    rows = D // (2 * lanes)
    which, core = lax.axis_index("k"), lax.axis_index("c")
    lane = lax.axis_index(("b", "x"))

    shard = rows // 2 + (0 if shared_edges else 1)

    def matrix(k):
        lines = []
        for place in range(2 * lanes):
            first = (2 * lanes * k + place) * shard
            columns = [full[pl.ds(first + at, rows // 8, D // 128)] for at in range(D // 128)]
            lines.append(jnp.concatenate([one.reshape(rows, 128) for one in columns], 1))
        return jnp.concatenate(lines, 0)

    def edge_table():
        lines = []
        for at in range(4 * lanes):
            even, odd = (full[(2 * at + one) * shard + shard - 1] for one in range(2))
            lines += [even[0:1], even[1:2] + odd[0:1], odd[1:2]]
        wide_lines = [jnp.concatenate(lines[4 * at : 4 * at + 4], 1) for at in range(12)]
        return jnp.concatenate(wide_lines + [jnp.zeros((4, D), F32)], 0)

    def start(copies):
        copies = [pltpu.make_async_copy(a, b, sems.at[at]) for at, (a, b) in enumerate(copies)]
        for one in copies:
            one.start()
        return copies

    copies = []
    for ref, segments in zip(pieces, layout):
        for plane, other, swapped, at, first, size in segments:
            place = (lane ^ other) * 2 + (core ^ swapped)
            to = ((which ^ plane) * 2 * lanes + place) * shard + first
            to = full.at[pl.ds(to, size)]
            copies.append((ref.at[pl.ds(at, size)], to))
    for one in start(copies):
        one.wait()
    for k in range(3):
        plain = matrix(k + 1)
        for (main, small, scales), one in ((wn, plain), (wt, plain.T)):
            scale = scale_of(largest(one))
            main[k], small[k, :, :D], small[k, :, D:] = parts(one, scale)
            scales[k : k + 1] = jnp.broadcast_to(1.0 / scale, (1, 128))
            reach = jnp.max(jnp.sum(jnp.abs(one.T if main is wn[0] else plain), 0, keepdims=True))
            scales[4 + k : 5 + k] = jnp.full((1, 128), reach, F32)
    edge = e_ref[...] if shared_edges else edge_table()
    table_ref[...] = edge
    row = lax.broadcasted_iota(jnp.int32, (8, D), 0)
    first = jnp.where(row < 7, edge[:8], 0.0)
    fh, fl = split(first)
    wh, wl = split(matrix(0))
    mixed = dot(fh, wh) + dot(fh, wl) + dot(fl, wh)
    biased = mixed + jnp.where(row == 6, edge[7:8], 0.0)
    columns = jnp.concatenate([edge[8:12], edge[3:6], mixed[3:6], jnp.zeros((118, D), F32)], 0).T
    for at in range(10):
        et[at] = jnp.broadcast_to(columns[:, at : at + 1], (D, 128))
    rows_of = [edge[:8], biased, edge[8:16], mixed]
    for at, part in enumerate(rows_of):
        limits[8 * at : 8 * at + 8] = jnp.broadcast_to(
            jnp.max(jnp.abs(part), 1, keepdims=True), (8, 128)
        )
    tang = jnp.where(row < 3, pltpu.roll(first, 5, 0), 0.0)
    tang_mixed = jnp.where(row < 3, pltpu.roll(mixed, 5, 0), 0.0)
    for at, part in enumerate((first, biased, tang, tang_mixed)):
        high, low = split(part)
        cat = jnp.concatenate(
            [high.astype(F32), high.astype(F32), low.astype(F32), jnp.zeros((104, D), F32)], 0
        ).T
        left[at] = cat.astype(BF16)

    def column(at):
        return lambda cut: jnp.concatenate([et[at, cut]] * (CHUNK // 128), 1)

    chunks = range(rcv_ref.shape[2] // CHUNK)
    blocks = [(at, one) for at in range(src_ref.shape[0]) for one in chunks]

    def each(stage, *lists):
        return [stage(*one) for one in zip(*lists)]

    def both(stage, *lists):
        return tuple(zip(*each(stage, *lists)))

    def triple(x):
        high, low = (part.astype(F32) for part in split(x))
        return jnp.concatenate([high, low, high, jnp.zeros((104, CHUNK), F32)], 0).astype(BF16)

    def points(step, b):
        lanes_of = slice(b * CHUNK, (b + 1) * CHUNK)
        near = near_ref[pl.ds(step, 1), lanes_of] == 1
        source = src_ref[step]
        p = [jnp.concatenate([source[j : j + 1]] * (CHUNK // 128), 1) for j in range(3)]
        raw = [rcv_ref[j, pl.ds(step, 1), lanes_of] for j in range(3)]
        q = [jnp.where(near, a + 0.1 * b, b) for a, b in zip(p, raw)]
        ends = [jnp.ones((1, CHUNK), F32), jnp.zeros((1, CHUNK), F32)]
        return jnp.concatenate(p + q + ends, 0)

    x = [points(*one) for one in blocks]
    vel = [vel_ref[pl.ds(at, 1), b * CHUNK : (b + 1) * CHUNK] for at, b in blocks]
    live = [live_ref[pl.ds(at, 1), b * CHUNK : (b + 1) * CHUNK].astype(F32) for at, b in blocks]
    x_wide = each(triple, x)
    h0 = each(lambda one: dot(left[0], one), x_wide)
    a0 = each(lambda one: dot(left[1], one), x_wide)

    def reach(weights, k, x):
        return weights[2][4 + k : 5 + k, 0:1] * x

    def limit(at):
        return limits[at : at + 1, 0:1]

    def over_rows(first, count, x):
        sizes = jnp.max(jnp.abs(x[:count]), 1, keepdims=True)
        return jnp.sum(limits[first : first + count, 0:1] * sizes, 0, keepdims=True)

    def graded(stage, bounds, *lists):
        def run(scale, *arrays):
            def one(*cut):
                x, *rest = stage(*cut)
                high, whole, left = parts(x, scale)
                top = jnp.max(jnp.abs(high).reshape(-1, 16, CHUNK), 0).astype(F32)
                return (high, whole, left, top, *rest)

            high, whole, left, top, *rest = tiles(one, *arrays)
            return (high, whole, left, scale), largest(top), *rest

        scale = scale_of(functools.reduce(jnp.maximum, bounds))
        return both(run, again(scale), *lists)

    def again(one):
        return [one] * len(blocks)

    def enter(c, bias):
        return elu_parts(c + bias)

    def add_half(c, bias, h):
        v, s, k = elu_parts(c + bias)
        return h + v, s, k

    u0s, top, s0, k0 = graded(elu_parts, each(lambda x: over_rows(8, 7, x), x), a0)
    c1 = each(lambda one: weigh(wt, 0, one), u0s)
    bounds = each(lambda x, top: over_rows(0, 7, x) + reach(wt, 0, top) + limit(16), x, top)
    h1s, top, s1, k1, h1 = graded(
        lambda *one: (lambda h, s, k: (h, s, k, h))(*add_half(*one)), bounds, c1, again(column(0)), h0
    )
    a2 = each(lambda one: weigh(wt, 1, one), h1s)
    bounds = each(lambda top: reach(wt, 1, top) + limit(17), top)
    u2s, _, s2, k2 = graded(enter, bounds, a2, again(column(1)))
    c3 = each(lambda one: weigh(wt, 2, one), u2s)

    def last_half(c, bias, h, e):
        h, s, k = add_half(c, bias, h)
        return s * e, h, s, k, sum_of(h * e)

    e_top = limit(19)
    y3, top, h2, s3, k3, out = graded(last_half, again(e_top), c3, again(column(2)), h1, again(column(3)))
    out = each(lambda one: jnp.sum(one, 0, keepdims=True), out)

    l2 = each(lambda one: weigh(wn, 2, one), y3)
    bounds = each(lambda top: reach(wn, 2, top), top)
    y2, top, q2 = graded(lambda l, s, k: (s * l, l * k), bounds, l2, s2, k2)
    l1 = each(lambda one: weigh(wn, 1, one), y2)
    bounds = each(lambda top: reach(wn, 1, top) + e_top, top)

    def back_add(value, e, s, k):
        value = value + e
        return s * value, value, value * k

    y1, _, lh1, q1 = graded(back_add, bounds, l1, again(column(3)), s1, k1)
    l0 = each(lambda one: weigh(wn, 0, one), y1)

    def leave(value, s, k, h, *columns):
        y = s * value
        sums = [sum_of(h * columns[j] + y * columns[3 + j]) for j in range(3)]
        return y, value * k, *sums

    y0, q0, *slope = both(
        lambda *one: tiles(leave, *one, *(column(4 + j) for j in range(6))), l0, s0, k0, lh1
    )
    slope = each(
        lambda *one: jnp.concatenate([jnp.sum(part, 0, keepdims=True) for part in one], 0), *slope
    )

    def loss_slopes(x, vel, live, out, slope):
        p, q = x[0:3], x[3:6]
        ratio = jnp.sqrt(out * out + 1.0)
        part = out / ratio
        off = q - p
        dist = jnp.sqrt(jnp.sum(off * off, 0, keepdims=True) + 0.01)
        unit = off / dist
        grad = ratio * unit + dist * part * slope
        size = jnp.sqrt(jnp.sum(grad * grad, 0, keepdims=True) + 0.01)
        misfit = vel * size - 1.0
        d_grad = (2.0 * live * misfit * vel / size) * grad
        d_slope = d_grad * (dist * part)
        d_ratio = jnp.sum(d_grad * unit, 0, keepdims=True)
        d_part = jnp.sum(d_grad * slope, 0, keepdims=True) * dist
        inv = 1.0 / ratio
        d_out = d_ratio * part + d_part * (inv * inv * inv)
        return d_out, jnp.concatenate([d_slope, jnp.zeros((5, CHUNK), F32)], 0)

    d_out, om = both(loss_slopes, x, vel, live, out, slope)
    om_wide = each(triple, om)
    t0 = each(lambda one: dot(left[2], one), om_wide)
    m0 = each(lambda one: dot(left[3], one), om_wide)

    bounds = each(lambda om: over_rows(27, 3, om), om)
    du0, top, q0 = graded(lambda m, s, q: (s * m, m * q), bounds, m0, s0, q0)
    n1 = each(lambda one: weigh(wt, 0, one), du0)
    bounds = each(lambda om, top: over_rows(3, 3, om) + reach(wt, 0, top), om, top)

    def along_add(n, t, s, q):
        t = t + s * n
        q = n * q
        return t, t, q, top_of(q)

    t1s, top, t1, q1, q1_top = graded(along_add, bounds, n1, t0, s1, q1)
    m2 = each(lambda one: weigh(wt, 1, one), t1s)

    def along(m, s, q):
        q = m * q
        return s * m, q, top_of(q)

    bounds = each(lambda top: reach(wt, 1, top), top)
    du2, top, q2, q2_top = graded(along, bounds, m2, s2, q2)
    n3 = each(lambda one: weigh(wt, 2, one), du2)

    def turn(n, s, k, t, h, e, d):
        cb = e * (d * s + n * k)
        return cb, fold(cb), fold(d * h + t + s * n)

    def down(u, s, q):
        ab = u * s + q
        return ab, fold(ab)

    def down_add(u, e, s, q, lh, d, x, om):
        hb = u + d * e
        cb = hb * s + q
        return cb, fold(cb), fold(hb), *weighted(hb, lh, x, om)

    def end(u, s, q, y, x, om):
        ab = u * s + q
        return fold(ab), *weighted(ab, y, x, om)

    def weighted(value, other, x, om):
        return [fold(value * x[3 + j : 4 + j] + other * om[j : j + 1]) for j in range(3)]

    def same(one):
        return lambda cut: one

    d_top = each(largest, d_out)
    d_all, x_all, om_all = (each(same, one) for one in (d_out, x, om))
    bounds = each(lambda d, top: e_top * (d + reach(wt, 2, top)), d_top, top)
    cb3, top, *sum3 = graded(turn, bounds, n3, s3, k3, t1, h2, again(column(3)), d_all)
    ub2 = each(lambda one: weigh(wn, 2, one), cb3)
    dw_ref[2] = outer((u2s, cb3), (du2, y3))
    bounds = each(lambda top, q: reach(wn, 2, top) + largest(q), top, q2_top)
    ab2, top, *sum2 = graded(down, bounds, ub2, s2, q2)
    hb1 = each(lambda one: weigh(wn, 1, one), ab2)
    dw_ref[1] = outer((h1s, ab2), (t1s, y2))
    bounds = each(lambda d, top, q: e_top * d + reach(wn, 1, top) + largest(q), d_top, top, q1_top)
    cb1, _, *sum1 = graded(down_add, bounds, hb1, again(column(3)), s1, q1, lh1, d_all, x_all, om_all)
    ub0 = each(lambda one: weigh(wn, 0, one), cb1)
    dw_ref[0] = outer((u0s, cb1), (du0, y1))
    sum0 = both(
        lambda u, s, q, y, a, b: tiles(end, u, s, q, y, same(a), same(b)), ub0, s0, q0, y0, x, om
    )
    for at, terms in enumerate((sum1[0], sum2[0], sum3[0], sum3[1])):
        sums[at] = sum(terms)
    for at, (ones, *points_of) in enumerate((sum0, sum1[1:])):
        wide[at, 6] = sum(ones)
        for j in range(3):
            wide[at, j] = sum(src_ref[one, j : j + 1] * part for (one, _), part in zip(blocks, ones))
            wide[at, 3 + j] = sum(points_of[j])

    copies = []
    size = rows // PARTS(lanes)
    for half, refs in ((1 - core, aways), (core, keeps)):
        for part in range(rows // size):
            for other in reversed(range(lanes)):
                first = pl.multiple_of((2 * (lane ^ other) + half) * rows + part * size, 8)
                for k in range(3):
                    there = refs[part * lanes + other].at[pl.ds(k * size, size)]
                    copies.append((dw_ref.at[k, pl.ds(first, size)], there))
    copies = start(copies)

    row = lax.broadcasted_iota(jnp.int32, (8, D), 0)

    def gather(at):
        lines = [jnp.sum(wide[at, one].T, 0, keepdims=True) for one in range(7)]
        return jnp.concatenate(lines + [jnp.zeros((1, D), F32)], 0)

    g, h = gather(0), gather(1)
    gh_, gl_ = split(g)
    wh, wl = split(matrix(0))
    first = h + dot(gh_, wh, NT) + dot(gh_, wl, NT) + dot(gl_, wh, NT)
    first = jnp.where(row < 7, first, g[6:7])
    tails = [jnp.sum(sums[at].T, 0, keepdims=True) for at in range(4)]
    small_ref[0:8] = first
    small_ref[8:16] = jnp.concatenate(tails + [jnp.zeros((4, D), F32)], 0)
    small_ref[16:24] = jnp.where(row < 7, g, 0.0)
    for one in copies:
        one.wait()


def pair_grads(pairs, edges, pieces, layout, lanes):
    rows = D // (2 * lanes)
    slots = lanes * PARTS(lanes)
    sent = [jax.ShapeDtypeStruct((3 * rows // PARTS(lanes), D), F32)] * (2 * slots)
    count = pairs[1].shape[1] * pairs[1].shape[2]
    segments = sum(len(one) for one in layout)
    vmem, held = pl.BlockSpec(memory_space=pltpu.VMEM), pl.BlockSpec(memory_space=pl.ANY)
    outs = pl.pallas_call(
        functools.partial(pair_kernel, layout, lanes),
        in_specs=[vmem] * (5 + len(edges)) + [held] * len(pieces),
        out_specs=[held] * len(sent) + [vmem] * 2,
        out_shape=sent
        + [jax.ShapeDtypeStruct((24, D), F32), jax.ShapeDtypeStruct((16, D), F32)],
        scratch_shapes=[
            pltpu.VMEM((3, D, D), F32),
            pltpu.VMEM((8 * lanes * (rows // 2 + (lanes == 4)), 8, 128), F32),
            pltpu.VMEM((4, D, 128), BF16),
            pltpu.VMEM((10, D, 128), F32),
            pltpu.VMEM((32, 128), F32),
            pltpu.VMEM((4, D, 128), F32),
            pltpu.VMEM((2, 7, D, 128), F32),
            pltpu.SemaphoreType.DMA((max(segments, 6 * slots),)),
        ]
        + [
            pltpu.VMEM((3, D, D), BF16),
            pltpu.VMEM((3, D, 2 * D), F8),
            pltpu.VMEM((8, 128), F32),
        ]
        * 2,
        compiler_params=pltpu.CompilerParams(vmem_limit_bytes=60 * 1024 * 1024),
        cost_estimate=pl.CostEstimate(
            flops=54 * 2 * count * D * D, bytes_accessed=8 * 1024 * 1024, transcendentals=4 * count * D
        ),
    )(*pairs, *edges, *pieces)
    return outs[:slots], outs[slots : 2 * slots], *outs[2 * slots :]


def adamw(weights, grads, first, second, rate):
    first_new = beta_one * first + (1.0 - beta_one) * grads
    second_new = beta_two * second + (1.0 - beta_two) * grads * grads
    first_hat = first_new / (1.0 - beta_one**ADAM_STEP)
    second_hat = second_new / (1.0 - beta_two**ADAM_STEP)
    weights_new = weights - rate * (
        first_hat / (jnp.sqrt(second_hat) + adam_eps) + decay_rate * weights
    )
    return (weights_new, first_new, second_new)


def exchange(x, plane, other, swapped, lanes):
    total = 8 * lanes
    mask = (plane * lanes + other) * 2 + swapped
    return lax.ppermute(x, AXES, [(i, i ^ mask) for i in range(total)])


def in_turn(first, *others):
    done = (first,)
    for one in others:
        one, *done = lax.optimization_barrier((one, *done))
        done = (*done, one)
    return done


def as_tiles(own):
    rows = own.shape[0]
    tiled = own.reshape(rows // 8, 8, D // 128, 128).transpose(0, 2, 1, 3)
    return tiled.reshape(rows // 2, 8, 128)


def spread(own, edges, sources, lanes):
    size = own.shape[0] // 2 + (lanes == 4)
    own = as_tiles(own)

    def at(plane, other, first=0):
        return [(plane, other, 0, first, 0, size)]

    def to_core(array):
        return exchange(array, 0, 0, 1, lanes)

    def to_place(array, other):
        return exchange(array, 0, other, 0, lanes)

    if lanes != 4:
        far = [exchange(own, plane, 0, 0, lanes) for plane in (1, 2, 3)]
        stack = jnp.concatenate([own] + far, 0)
        got = [
            (to_place(stack, other) if other else stack, sum((at(p, other, p * size) for p in range(4)), []))
            for other in range(lanes)
        ]
        swaps = [to_core(array) for array, _ in got]
    else:
        odd = lax.axis_index("c") == 1
        line = jnp.where(odd, jnp.pad(edges, (64, 0)), jnp.pad(edges, (0, 64)))
        line = jnp.pad(line.reshape(1, 2, 128), ((0, 0), (0, 6), (0, 0)))
        own = jnp.concatenate([own, line], 0)
        far = [exchange(own, plane, 0, 0, lanes) for plane in (1, 2, 3)]
        near = [to_place(own, other) for other in (1, 2)]
        diagonal = to_place(own, 3)
        far[0], sources, far[1], far[2], near[1], near[0], diagonal = in_turn(
            far[0], sources, far[1], far[2], near[1], near[0], diagonal
        )
        early = [own, *near, diagonal]
        stack = jnp.concatenate(far, 0)
        more = [to_place(stack, other) for other in (1, 2)]
        swaps = [to_core(array) for array in early[:3]]
        ahead = more[1]
        more[1], more[0], *swaps = in_turn(more[1], more[0], *swaps)
        half = 3 * size // 2
        ends = [to_place(ahead[:half], 1), to_place(more[0][half:], 2)]
        swaps += [to_core(array) for array in (diagonal, stack, *more)]
        tied = in_turn(*ends, *swaps)
        ends, swaps = tied[:2], list(tied[2:])

        def three(other):
            return sum((at(p, other, (p - 1) * size) for p in (1, 2, 3)), [])

        def cut(segments, low, high):
            found = []
            for plane, other, core, here, first, count in segments:
                start, stop = max(here, low), min(here + count, high)
                if start < stop:
                    found.append((plane, other, core, start - low, first + start - here, stop - start))
            return found

        got = [(array, at(0, other)) for other, array in enumerate(early)]
        got += [(stack, three(0)), (more[0], three(1)), (more[1], three(2))]
        got += [(ends[0], cut(three(3), 0, half)), (ends[1], cut(three(3), half, 3 * size))]
        swaps += [to_core(array) for array in ends]
    got += [
        (array, [(a, b, 1, *rest) for a, b, _, *rest in segments])
        for array, (_, segments) in zip(swaps, list(got))
    ]
    return [array for array, _ in got], [tuple(segments) for _, segments in got], sources


def local(
    lanes,
    src_coords,
    rcv_coords,
    velocity,
    pair_mask,
    near_flag,
    block_params,
    edge_params,
    block_moment,
    edge_moment,
    block_second,
    edge_second,
):
    plane = 2 * lanes
    total = 4 * plane
    rows = block_params.shape[0]
    which, core = lax.axis_index("k"), lax.axis_index("c")
    me = lax.axis_index(AXES)

    def to_all(x):
        return lax.all_to_all(x, AXES, 0, 0, tiled=True)

    share = edge_params.shape[0]
    sources = jnp.broadcast_to(src_coords.T.reshape(-1, 3, 1), (src_coords.shape[1], 3, 128))
    edges = []
    if lanes != 4:
        edges = to_all(jnp.broadcast_to(edge_params[None, None], (total, 1, share)))
        edges = [jnp.pad(edges.reshape(12, D), ((0, 4), (0, 0)))]
    pieces, layout, sources = spread(block_params, edge_params, sources, lanes)
    pairs = (sources, rcv_coords, velocity, pair_mask, near_flag)
    away, keep, small, edges = pair_grads(pairs, edges, pieces, layout, lanes)

    arrived = []
    for at in range(PARTS(lanes)):
        got = []
        for other in reversed(range(lanes)):
            slot = at * lanes + other
            part = keep[slot] + exchange(away[slot], 0, 0, 1, lanes)
            got.append(exchange(part, 0, other, 0, lanes) if other else part)
        arrived.append([*in_turn(*got[:-1]), got[-1]])
    shares = [small[:12].reshape(total, 1, share), small[16:24].reshape(FACTORS, 1, -1)]
    shares[1] = jnp.pad(shares[1], ((0, total - FACTORS), (0, 0), (0, 0)))
    shares = to_all(jnp.concatenate(shares, 2))

    arrived[-1][0], shares = lax.optimization_barrier((arrived[-1][0], shares))
    owned = []
    for terms in arrived:
        size = rows // PARTS(lanes)

        def rows_of(matrix):
            at = jnp.maximum(matrix - 1, 0) * size
            return sum(lax.dynamic_slice_in_dim(one, at, size, 0) for one in terms)

        for other in (3, 2, 1):
            perm = [(i, i ^ (other * plane)) for i in range(total)]
            owned.append(lax.ppermute(rows_of(which ^ other), AXES, perm))
        owned.append(rows_of(which))
    ahead = in_turn(*(one for at, one in enumerate(owned) if at % 4 != 3))
    owned = [x for at in range(0, len(ahead), 3) for x in (*ahead[at : at + 3], owned[at // 3 * 4 + 3])]

    kind = which.astype(jnp.int32).reshape(1)
    owned, own_edges, shared = collect(kind, owned, shares, pair_mask, share)
    shared = to_all(shared)
    own_first = lax.dynamic_slice_in_dim(edges[:8], me % plane * rows, rows, 1).T
    return update(
        kind,
        (shared, edges[:8], own_first),
        (owned, block_params, block_moment, block_second),
        (own_edges, edge_params, edge_moment, edge_second),
    )


def collect_kernel(kind_ref, shares_ref, mask_ref, *refs):
    owned_ref, edges_ref, shared_ref = refs[-3:]
    share = edges_ref.shape[1]
    kind = kind_ref[0]

    terms = refs[:-3]
    size = terms[0].shape[0]
    for at in range(len(terms) // 4):
        total = sum(one[...] for one in terms[4 * at : 4 * at + 4])
        owned_ref[at * size : (at + 1) * size] = jnp.where(kind == 0, 0.0, total)
    shares = jnp.sum(shares_ref[...], 0)
    own = shares[:, :share]
    edges_ref[...] = own

    def whole(x):
        return jnp.sum(jnp.sum(x, 0, keepdims=True), 1, keepdims=True)

    squares = whole(owned_ref[...] * owned_ref[...]) + whole(own * own)
    live = whole(mask_ref[...].astype(F32))
    lane = lax.broadcasted_iota(jnp.int32, (1, 128), 1)
    sums = jnp.where(lane == 0, squares, jnp.where(lane == 1, live, 0.0))
    line = jnp.concatenate([sums, shares[:, share:]], 1)
    shared_ref[...] = jnp.broadcast_to(line[None], shared_ref.shape)


def collect(kind, owned, shares, mask, share):
    rows, total = owned[0].shape[0] * (len(owned) // 4), shares.shape[0]
    smem, vmem = pl.BlockSpec(memory_space=pltpu.SMEM), pl.BlockSpec(memory_space=pltpu.VMEM)
    shapes = [(rows, D), (1, share), (total, 1, 256)]
    return pl.pallas_call(
        collect_kernel,
        in_specs=[smem] + [vmem] * (2 + len(owned)),
        out_specs=[vmem] * 3,
        out_shape=[jax.ShapeDtypeStruct(one, F32) for one in shapes],
        compiler_params=SMALL,
    )(kind, shares, mask, *owned)


def update_kernel(kind_ref, shared_ref, edge_ref, own_ref, *refs):
    ins, outs = refs[:8], refs[8:]
    shared = jnp.sum(shared_ref[:, :, :128], 0)
    lane = lax.broadcasted_iota(jnp.int32, shared.shape, 1)
    per = D // 128
    lines = [
        jnp.concatenate([shared_ref[at * per + one, :, 128:] for one in range(per)], 1)
        for at in range(8)
    ]
    factor, rows, own = jnp.concatenate(lines, 0), edge_ref[...], own_ref[...]
    first = jnp.zeros(ins[0].shape, F32)
    mixed = jnp.zeros_like(factor)
    for at in range(7):
        first = first + own[:, at : at + 1] * factor[at : at + 1]
        gram = jnp.sum(rows * rows[at : at + 1], 1, keepdims=True)
        mixed = mixed + gram * factor[at : at + 1]
    valid = lax.broadcasted_iota(jnp.int32, factor.shape, 0) < 7
    first_sq = jnp.sum(jnp.where(valid, mixed * factor, 0.0), 0, keepdims=True)
    first_sq = jnp.sum(first_sq, 1, keepdims=True)
    total_sq = jnp.sum(jnp.where(lane == 0, shared, 0.0), 1, keepdims=True) + first_sq
    count = jnp.sum(jnp.where(lane == 1, shared, 0.0), 1, keepdims=True)
    count = jnp.maximum(count, 1.0)
    grad_norm = jnp.sqrt(total_sq) / count
    outs[0][0] = grad_norm[0, 0]
    scale = jnp.minimum(1.0, clip_limit / (grad_norm + 1e-06)) / count
    for at, rate in ((0, block_rate), (4, edge_rate)):
        raw, weights, one, two = (ref[...] for ref in ins[at : at + 4])
        if at == 0:
            raw = jnp.where(kind_ref[0] == 0, first, raw)
        weights, one, two = adamw(weights, raw * scale, one, two, rate)
        outs[1 + at][...] = weights
        outs[2 + at][...] = one
        outs[3 + at][...] = two
        low = weights.astype(BF16)
        outs[4 + at][...] = low.reshape(outs[4 + at].shape)


def update(kind, shared, blocks, edges):
    edges = (edges[0],) + tuple(one[None] for one in edges[1:])
    smem, vmem = pl.BlockSpec(memory_space=pltpu.SMEM), pl.BlockSpec(memory_space=pltpu.VMEM)
    shapes = [(1,)] + [blocks[0].shape] * 4 + [edges[0].shape] * 3 + [edges[0].shape[1:]]
    types = [F32] + [F32, F32, F32, BF16] * 2
    outs = pl.pallas_call(
        update_kernel,
        in_specs=[smem] + [vmem] * 11,
        out_specs=[smem] + [vmem] * 8,
        out_shape=[jax.ShapeDtypeStruct(a, b) for a, b in zip(shapes, types)],
        compiler_params=SMALL,
    )(kind, *shared, *blocks, *edges)
    norm, new_b, moment_b, second_b, low_b, new_e, moment_e, second_e, low_e = outs
    new_e, moment_e, second_e = (one[0] for one in (new_e, moment_e, second_e))
    return norm.reshape(()), new_b, new_e, moment_b, moment_e, second_b, second_e, low_b, low_e


def solution(mesh):
    count_src, count_rcv = mesh.shape["src"], mesh.shape["rcv"]
    shape = (4, count_src // 4, count_rcv // 2, 2)
    split_mesh = jax.sharding.Mesh(mesh.devices.reshape(shape), AXES)
    src, rcv = ("k", "b"), ("x", "c")
    wide, flat = P(AXES, None), P(AXES)
    placed = (
        P(None, src),
        P(None, src, rcv),
        P(src, rcv),
        P(src, rcv),
        P(src, rcv),
        wide,
        flat,
        wide,
        flat,
        wide,
        flat,
    )
    return jax.shard_map(
        functools.partial(local, shape[1] * shape[2]),
        mesh=split_mesh,
        in_specs=placed,
        out_specs=(P(), wide, flat, wide, flat, wide, flat, wide, flat),
        check_vma=False,
    )
```
